512 devices in a mesh: grp: 16 (over x, y_lo, core), wide: 32 (over z, y_hi).
Axes of the slice: x: 4, y: 8 (y_hi: 4, y_lo: 2; y = y_hi * 2 + y_lo), z: 8, core: 2. Of those that a mesh axis runs over, the one named last changes fastest.
Arguments:
- queries: bfloat16 [2, 4, 128, 576], replicated
- cache: bfloat16 [2, 1048576, 576], P(None, ('grp', 'wide'))
- lengths: int32 [2], replicated, may hold values from 128 to 1048576, as said below
- up_weight: bfloat16 [128, 512, 128], P('grp'), may hold values from -0.25 to 0.25
- out_weight: bfloat16 [16384, 7168], P('grp', 'wide'), may hold values from -0.046875 to 0.046875
Outputs:
- mixed: float32 [2, 4, 7168], P(None, None, 'wide')
The draws below stay inside these ranges and needn't reach their ends.
Inputs may be any that keep to these rules, and one draw needn't show every extreme that they name: `lengths`: multiples of 128; one sequence fills all 1048576 positions, the other is shorter.
All inputs are finite; a program needn't handle non-finite values.
Results may differ from the reference program's by a relative error of at most 0.00085.
Values sent between devices are 32-bit elements; how exact they have to be, the bound alone decides.
No kernel may reach another device: no remote copies, remote signals or barrier semaphores. Data moves between devices by JAX's collectives and lax.ppermute only.
A program may use at most 128 MiB of HBM per device.

```python
import math
import jax
import jax.numpy as jnp
from jax import lax

HEAD_COUNT = 128
LATENT = 512
VALUE_DIM = 128
DMODEL = 7168
BATCH_ROWS = 2
QUERIES = 4
CTX_DEV = 2048
ENTRY_WIDTH = 576
CONTEXT = 1048576


def common_parts(key):
    keys = jax.random.split(key, 2)
    channel_mean = jax.random.normal(keys[0], (ENTRY_WIDTH,), jnp.float32)
    offsets = 2.5 * jax.random.normal(keys[1], (BATCH_ROWS, CONTEXT // 128, ENTRY_WIDTH), jnp.float32)
    base = channel_mean + jnp.repeat(offsets, 128, axis=1)
    return base


def draw_cache(key, part):
    base = common_parts(key)
    key = jax.random.fold_in(key, 3)
    entries = base + jax.random.normal(key, base.shape, jnp.float32)
    return entries.astype(jnp.bfloat16)


def draw_queries(key, part):
    key = jax.random.fold_in(key, 5)
    keys = jax.random.split(key, 1)
    shape = (BATCH_ROWS, QUERIES, HEAD_COUNT, ENTRY_WIDTH)
    entries = 0.2 * jax.random.normal(keys[0], shape, jnp.float32)
    return entries.astype(jnp.bfloat16)


def draw_lengths(key, part):
    key = jax.random.fold_in(key, 7)
    keys = jax.random.split(key, 2)
    other = 128 * jax.random.randint(keys[0], (), 1, CONTEXT // 128)
    full = jnp.full((), CONTEXT, jnp.int32)
    flip = jax.random.randint(keys[1], (), 0, 2)
    return jnp.where(flip == 0, jnp.stack([full, other]), jnp.stack([other, full])).astype(jnp.int32)


def block_levels(own_key, extent, cuts, low, high):
    loudness = 1.0
    for axis_at, shards_of in cuts:
        steps = jax.random.uniform(jax.random.fold_in(jax.random.fold_in(own_key, 6), axis_at), (shards_of,), jnp.float32, low / len(cuts), high / len(cuts))
        loudness = loudness * jnp.repeat(jnp.exp(steps), extent[axis_at] // shards_of).reshape((-1,) + (1,) * (len(extent) - 1 - axis_at))
    return loudness


def gaussian(stream_key, extent, spread, most, cuts=(), held_as=jnp.bfloat16):
    level = block_levels(stream_key, extent, cuts, -0.22, 0.18) if cuts else 1.0
    values = jax.random.normal(stream_key, extent, jnp.float32) * spread * level
    return jnp.minimum(jnp.maximum(values, -most), most).astype(held_as)


def setup_inputs(seed: int = 0) -> dict:
    seeds = jax.random.split(jax.random.key(seed), 6)
    return {
        "queries": draw_queries(jax.random.fold_in(seeds[5], 71), 0),
        "cache": draw_cache(jax.random.fold_in(seeds[5], 71), 0),
        "lengths": draw_lengths(jax.random.fold_in(seeds[5], 71), 0),
        "up_weight": gaussian(seeds[3], (HEAD_COUNT, LATENT, VALUE_DIM), LATENT ** -0.5, 0.25, ((0, 16),)),
        "out_weight": gaussian(seeds[4], (HEAD_COUNT * VALUE_DIM, DMODEL), (HEAD_COUNT * VALUE_DIM) ** -0.5, 0.046875, ((0, 16), (1, 32))),
    }


softmax_factor = 1.0 / math.sqrt(192.0) * (0.1 * math.log(40.0) + 1.0) ** 2
floor_value = -1e+30

def combine(first, second_part):
    acc_a, top_a, total_a = first
    acc_b, top_b, total_b = second_part
    peak = jnp.maximum(top_a, top_b)
    scale_a = jnp.exp(top_a - peak)
    scale_b = jnp.exp(top_b - peak)
    return (acc_a * scale_a[..., None] + acc_b * scale_b[..., None], peak, total_a * scale_a + total_b * scale_b)

def reference(queries, cache, lengths, up_weight, out_weight):
    blocks = CONTEXT // CTX_DEV
    flattened = queries.reshape(BATCH_ROWS, QUERIES * HEAD_COUNT, ENTRY_WIDTH).astype(jnp.float32)
    query_pos = (jnp.arange(QUERIES * HEAD_COUNT, dtype=jnp.int32) // HEAD_COUNT).astype(jnp.int32)
    limits = lengths[:, None] - QUERIES + 1 + query_pos[None, :]

    def step(carry, index):
        start = (index * CTX_DEV).astype(jnp.int32)
        cache_block = lax.dynamic_slice_in_dim(cache, start, CTX_DEV, 1).astype(jnp.float32)
        logit_scores = jnp.einsum('ond,ovd->onv', flattened, cache_block, precision=lax.Precision.HIGHEST) * softmax_factor
        positions = start + jnp.arange(CTX_DEV, dtype=jnp.int32)
        visible = positions[None, None, :] < limits[:, :, None]
        local = lax.optimization_barrier(jnp.max(jnp.where(visible, logit_scores, floor_value), axis=-1))
        weights = jnp.where(visible, jnp.exp(logit_scores - local[..., None]), 0.0).astype(jnp.bfloat16)
        wide_weights = weights.astype(jnp.float32)
        total = lax.optimization_barrier(jnp.sum(wide_weights, axis=-1))
        acc = jnp.einsum('bqs,bsc->bqc', wide_weights, cache_block[:, :, :LATENT], precision=lax.Precision.HIGHEST)
        return (combine(carry, (acc, local, total)), None)
    start_state = (jnp.zeros((BATCH_ROWS, QUERIES * HEAD_COUNT, LATENT), jnp.float32), jnp.full((BATCH_ROWS, QUERIES * HEAD_COUNT), floor_value, jnp.float32), jnp.zeros((BATCH_ROWS, QUERIES * HEAD_COUNT), jnp.float32))
    (acc, peak, total), unused = lax.scan(step, start_state, jnp.arange(blocks, dtype=jnp.int32))
    latent_out = (acc / total[..., None]).reshape(BATCH_ROWS * QUERIES, HEAD_COUNT, LATENT)
    values = jnp.einsum('rhc,hcv->rhv', latent_out, up_weight.astype(jnp.float32), precision=lax.Precision.HIGHEST)
    mixed = jnp.dot(values.reshape(BATCH_ROWS * QUERIES, HEAD_COUNT * VALUE_DIM), out_weight.astype(jnp.float32), precision=lax.Precision.HIGHEST)
    return mixed.reshape(BATCH_ROWS, QUERIES, DMODEL)
```

```python
import math

import jax
import jax.numpy as jnp
from jax import lax
from jax.experimental import pallas as pl
from jax.experimental.pallas import tpu as pltpu
from jax.sharding import PartitionSpec as P

softmax_factor = 1.0 / math.sqrt(192.0) * (0.1 * math.log(40.0) + 1.0) ** 2
score_scale = softmax_factor * math.log2(math.e)
floor_value = -1e30
floor_guard = -5e29

LANES = 128
SUB = 8


def split_dot(x, w, contract=0):
    rows = x.shape[0]
    high = x.astype(jnp.bfloat16)
    low = (x - high.astype(jnp.float32)).astype(jnp.bfloat16)
    both = lax.dot_general(jnp.concatenate([high, low], axis=0), w, (((1,), (contract,)), ((), ())),
                           preferred_element_type=jnp.float32)
    return both[:rows] + both[rows:]


def attend(queries, cache, lengths, groups, latent):
    rows, draft, key_dim, heads = queries.shape
    span = cache.shape[2]
    owned = heads // groups
    pairs = groups // 2
    lat_tiles = latent // LANES
    count = rows * draft
    tiles = count * lat_tiles + 1
    qrows = draft * heads

    def kernel(q_hbm, cache_hbm, len_ref, keep_hbm, send_hbm,
               q_v, k_v, s_v, acc_v, top_v, tot_v, stat_v, q_sem, k_sem, out_sem):
        grp = lax.axis_index("grp")
        core = lax.rem(grp, 2)
        start = (grp * lax.axis_size("wide") + lax.axis_index("wide")) * span
        q_copies = [pltpu.make_async_copy(q_hbm.at[b], q_v.at[b], q_sem.at[b]) for b in range(rows)]
        k_copies = [pltpu.make_async_copy(cache_hbm.at[b], k_v.at[b], k_sem.at[b]) for b in range(rows)]
        for b in range(rows):
            q_copies[b].start()
            k_copies[b].start()
        out_copies = []

        def send_out(view, tile_at, n_tiles, slot):
            for i, (dst, flip) in enumerate(((send_hbm, 1), (keep_hbm, 0))):
                copy = pltpu.make_async_copy(
                    view(jnp.bitwise_xor(core, flip)), dst.at[:, pl.ds(tile_at, n_tiles)], out_sem.at[i, slot])
                copy.start()
                out_copies.append(copy)

        pos = start + lax.broadcasted_iota(jnp.int32, (1, span), 1)
        for b in range(rows):
            q_copies[b].wait()
            k_copies[b].wait()
            tops = []
            for j in range(draft):
                s = lax.dot_general(q_v[b, j], k_v[b], (((0,), (0,)), ((), ())),
                                    preferred_element_type=jnp.float32) * score_scale
                s = jnp.where(pos < len_ref[b] - draft + 1 + j, s, floor_value)
                s_v[b, j * heads:(j + 1) * heads, :] = s
                running = s[:, :LANES]
                for c in range(1, span // LANES):
                    running = jnp.maximum(running, s[:, c * LANES:(c + 1) * LANES])
                tops.append(running)
            top = jnp.max(jnp.concatenate(tops, axis=0), axis=-1, keepdims=True)
            top_v[b] = jnp.broadcast_to(top, (qrows, LANES))
            w = jnp.exp2(s_v[b] - jnp.maximum(top, floor_guard)).astype(jnp.bfloat16)
            wide_w = w.astype(jnp.float32)
            total = wide_w[:, :LANES]
            for c in range(1, span // LANES):
                total = total + wide_w[:, c * LANES:(c + 1) * LANES]
            acc = lax.dot_general(w, k_v[b, :latent, :], (((1,), (1,)), ((), ())),
                                  preferred_element_type=jnp.float32)
            tot_v[b] = jnp.broadcast_to(jnp.sum(total, axis=-1, keepdims=True), (qrows, LANES))
            for j in range(draft):
                block = acc[j * heads:(j + 1) * heads].reshape(pairs, 2, owned, latent)
                for c in range(lat_tiles):
                    acc_v[b, j, :, :, c] = block[:, :, :, c * LANES:(c + 1) * LANES]
            for j in range(draft):
                r = b * draft + j
                send_out(lambda bit: acc_v.at[b, j, :, bit], r * lat_tiles, lat_tiles, r)
        lane = lax.broadcasted_iota(jnp.int32, (owned, LANES), 1)
        for g in range(groups):
            stat = jnp.zeros((owned, LANES), jnp.float32)
            for r in range(count):
                b, j = r // draft, r % draft
                at = slice(j * heads + g * owned, j * heads + (g + 1) * owned)
                stat = jnp.where(lane == r, top_v[b, at, :], stat)
                stat = jnp.where(lane == count + r, tot_v[b, at, :], stat)
            stat_v[g // 2, g % 2, 0] = stat
        send_out(lambda bit: stat_v.at[:, bit], tiles - 1, 1, count)
        for copy in out_copies:
            copy.wait()

    message = jax.ShapeDtypeStruct((pairs, tiles, owned, LANES), jnp.float32)
    any_space = pl.BlockSpec(memory_space=pl.ANY)
    return pl.pallas_call(
        kernel,
        out_shape=(message, message),
        in_specs=[any_space, any_space, pl.BlockSpec(memory_space=pltpu.SMEM)],
        out_specs=(any_space, any_space),
        scratch_shapes=[
            pltpu.VMEM((rows, draft, key_dim, heads), jnp.bfloat16),
            pltpu.VMEM((rows, key_dim, span), jnp.bfloat16),
            pltpu.VMEM((rows, qrows, span), jnp.float32),
            pltpu.VMEM((rows, draft, pairs, 2, lat_tiles, owned, LANES), jnp.float32),
            pltpu.VMEM((rows, qrows, LANES), jnp.float32),
            pltpu.VMEM((rows, qrows, LANES), jnp.float32),
            pltpu.VMEM((pairs, 2, 1, owned, LANES), jnp.float32),
            pltpu.SemaphoreType.DMA((rows,)),
            pltpu.SemaphoreType.DMA((rows,)),
            pltpu.SemaphoreType.DMA((2, count + 1)),
        ],
        compiler_params=pltpu.CompilerParams(vmem_limit_bytes=63 << 20),
        name="attend",
    )(queries, cache, lengths)


def fold_stats(stats, count):
    peak = stats[0]
    for s in stats[1:]:
        peak = jnp.maximum(peak, s)
    scales = [jnp.exp2(s - peak) for s in stats]
    total = None
    for s, e in zip(stats, scales):
        part = pltpu.roll(s, LANES - count, 1) * e
        total = part if total is None else total + part
    lane = lax.broadcasted_iota(jnp.int32, peak.shape, 1)
    joint = jnp.where(lane < count, peak, pltpu.roll(total, count, 1))
    return scales, total, jnp.where(lane < 2 * count, joint, 0.0)


def add_cores(keep, other, count):
    pairs, tiles = keep.shape[:2]
    per = (tiles - 1) // count

    def kernel(a_ref, b_ref, o_ref):
        for a in range(a_ref.shape[0]):
            scales, _, joint = fold_stats([a_ref[a, tiles - 1], b_ref[a, tiles - 1]], count)
            o_ref[a, tiles - 1] = joint
            for r in range(count):
                ea = scales[0][:, r:r + 1]
                eb = scales[1][:, r:r + 1]
                for c in range(per):
                    t = r * per + c
                    o_ref[a, t] = a_ref[a, t] * ea + b_ref[a, t] * eb

    steps = 4
    spec = pl.BlockSpec((pairs // steps,) + keep.shape[1:], lambda i: (i, 0, 0, 0))
    return pl.pallas_call(
        kernel,
        grid=(steps,),
        out_shape=jax.ShapeDtypeStruct(keep.shape, jnp.float32),
        in_specs=[spec, spec],
        out_specs=spec,
        compiler_params=pltpu.CompilerParams(vmem_limit_bytes=32 << 20),
        name="add_cores",
    )(keep, other)


def up_project(parts, up_weight, count, copies):
    sources, tiles = parts.shape[:2]
    owned, latent, value_dim = up_weight.shape
    per = (tiles - 1) // count

    def kernel(p_ref, u_ref, o_ref, lat_v):
        scales, _, joint = fold_stats([p_ref[s, tiles - 1] for s in range(sources)], count)
        for r in range(count):
            es = [jnp.broadcast_to(e[:, r:r + 1], (SUB, LANES)) for e in scales]
            for c in range(per):
                t = r * per + c
                total = p_ref[0, t] * es[0]
                for s in range(1, sources):
                    total = total + p_ref[s, t] * es[s]
                lat_v[c, r * SUB:(r + 1) * SUB, :] = total
        row = lax.broadcasted_iota(jnp.int32, (count * SUB, value_dim), 0) % SUB
        lat = jnp.concatenate([lat_v[c] for c in range(per)], axis=1)
        values = jnp.zeros((count * SUB, value_dim), jnp.float32)
        for h in range(owned):
            values = jnp.where(row == h, split_dot(lat, u_ref[h]), values)
        for i in range(copies):
            for r in range(count):
                o_ref[i, r] = values[r * SUB:(r + 1) * SUB]
            o_ref[i, count] = joint

    return pl.pallas_call(
        kernel,
        out_shape=jax.ShapeDtypeStruct((copies, count + 1, SUB, LANES), jnp.float32),
        scratch_shapes=[pltpu.VMEM((per, count * SUB, LANES), jnp.float32)],
        compiler_params=pltpu.CompilerParams(vmem_limit_bytes=32 << 20),
        name="up_project",
    )(parts, up_weight)


def add_wide(parts, count, copies):
    sources = parts.shape[0]

    def kernel(p_ref, o_ref):
        scales, _, joint = fold_stats([p_ref[s, count] for s in range(sources)], count)
        for r in range(count):
            value = None
            for s in range(sources):
                part = p_ref[s, r] * scales[s][:, r:r + 1]
                value = part if value is None else value + part
            for i in range(copies):
                o_ref[i, r] = value
        for i in range(copies):
            o_ref[i, count] = joint

    return pl.pallas_call(
        kernel,
        out_shape=jax.ShapeDtypeStruct((copies,) + parts.shape[1:], jnp.float32),
        compiler_params=pltpu.CompilerParams(vmem_limit_bytes=32 << 20),
        name="add_wide",
    )(parts)


def out_project(parts, out_weight, count, copies):
    sources = parts.shape[0]
    features = out_weight.shape[0]

    def kernel(p_ref, w_ref, o_ref, val_v):
        scales, total, _ = fold_stats([p_ref[s, count] for s in range(sources)], count)
        inverse = 1.0 / total
        for r in range(count):
            value = None
            for s in range(sources):
                part = p_ref[s, r] * scales[s][:, r:r + 1]
                value = part if value is None else value + part
            val_v[r * SUB:(r + 1) * SUB, :] = value * inverse[:, r:r + 1]
        values = jnp.concatenate([val_v[pl.ds(h, count, stride=SUB), :] for h in range(SUB)], axis=1)
        mixed = split_dot(values, w_ref[...], 1)
        for i in range(copies):
            o_ref[i] = mixed

    return pl.pallas_call(
        kernel,
        out_shape=jax.ShapeDtypeStruct((copies, count, features), jnp.float32),
        scratch_shapes=[pltpu.VMEM((count * SUB, LANES), jnp.float32)],
        compiler_params=pltpu.CompilerParams(vmem_limit_bytes=32 << 20),
        name="out_project",
    )(parts, out_weight)


def body(queries, cache, lengths, up_weight, out_weight):
    rows, draft = queries.shape[:2]
    count = rows * draft
    groups = lax.axis_size("grp")
    wide = lax.axis_size("wide")
    near = 4
    same_core = [list(range(c, groups, 2)) for c in range(2)]
    along_y = [list(range(z, z + near)) for z in range(0, wide, near)]
    along_z = [list(range(y, wide, near)) for y in range(near)]
    keep, send = attend(jnp.swapaxes(queries, 2, 3), jnp.swapaxes(cache, 1, 2), lengths, groups, up_weight.shape[1])
    other = lax.ppermute(send, "grp", [(i, i ^ 1) for i in range(groups)])
    mine = add_cores(keep, other, count)
    parts = lax.all_to_all(mine, "grp", 0, 0, axis_index_groups=same_core, tiled=True)
    values = up_project(parts, up_weight, count, near)
    values = lax.all_to_all(values, "wide", 0, 0, axis_index_groups=along_y, tiled=True)
    values = add_wide(values, count, wide // near)
    values = lax.all_to_all(values, "wide", 0, 0, axis_index_groups=along_z, tiled=True)
    mixed = out_project(values, out_weight.T, count, groups)
    mixed = lax.all_to_all(mixed, "grp", 0, 0, tiled=True)
    return jnp.sum(mixed, axis=0).reshape(rows, draft, mixed.shape[2])


def solution(mesh):
    in_specs = (P(), P(None, ("grp", "wide"), None), P(), P("grp", None, None), P("grp", "wide"))
    out_specs = P(None, None, "wide")
    return jax.shard_map(body, mesh=mesh, in_specs=in_specs, out_specs=out_specs, check_vma=False)
```

```python
import math

import jax
import jax.numpy as jnp
from jax import lax
from jax.experimental import pallas as pl
from jax.experimental.pallas import tpu as pltpu
from jax.sharding import PartitionSpec as P

softmax_factor = 1.0 / math.sqrt(192.0) * (0.1 * math.log(40.0) + 1.0) ** 2
score_scale = softmax_factor * math.log2(math.e)
floor_value = -1e30
floor_guard = -5e29

LANES = 128
SUB = 8
FIRST_PARTS = 2


def split_dot(x, w, contract=0):
    rows = x.shape[0]
    high = x.astype(jnp.bfloat16)
    low = (x - high.astype(jnp.float32)).astype(jnp.bfloat16)
    both = lax.dot_general(jnp.concatenate([high, low], axis=0), w, (((1,), (contract,)), ((), ())),
                           preferred_element_type=jnp.float32)
    return both[:rows] + both[rows:]


def attend(queries, cache, lengths, groups, latent):
    rows, draft, key_dim, heads = queries.shape
    span = cache.shape[2]
    owned = heads // groups
    pairs = groups // 2
    lat_tiles = latent // LANES
    count = rows * draft
    tiles = count * lat_tiles + 1
    qrows = draft * heads

    def pieces(b):
        part = span // FIRST_PARTS if b == 0 else span
        return [(lo, lo + part) for lo in range(0, span, part)]

    def kernel(q_hbm, cache_hbm, len_ref, keep_ref, send_ref,
               q_v, k_v, s_v, acc_v, top_v, tot_v, stat_v, q_sem, k_sem):
        grp = lax.axis_index("grp")
        core = lax.rem(grp, 2)
        start = (grp * lax.axis_size("wide") + lax.axis_index("wide")) * span
        q_copies = [pltpu.make_async_copy(q_hbm.at[b], q_v.at[b], q_sem.at[b]) for b in range(rows)]
        k_copies = [
            [pltpu.make_async_copy(cache_hbm.at[b, :, pl.ds(lo, hi - lo)], k_v.at[b, :, pl.ds(lo, hi - lo)], k_sem.at[b, p])
             for p, (lo, hi) in enumerate(pieces(b))] for b in range(rows)]
        for b in range(rows):
            q_copies[b].start()
            for copy in k_copies[b]:
                copy.start()
        for b in range(rows):
            q_copies[b].wait()
            tops = [None] * draft
            for copy, (lo, hi) in zip(k_copies[b], pieces(b)):
                copy.wait()
                pos = start + lo + lax.broadcasted_iota(jnp.int32, (1, hi - lo), 1)
                for j in range(draft):
                    s = lax.dot_general(q_v[b, j], k_v[b, :, lo:hi], (((0,), (0,)), ((), ())),
                                        preferred_element_type=jnp.float32) * score_scale
                    s = jnp.where(pos < len_ref[b] - draft + 1 + j, s, floor_value)
                    s_v[b, j * heads:(j + 1) * heads, lo:hi] = s
                    for c in range((hi - lo) // LANES):
                        piece = s[:, c * LANES:(c + 1) * LANES]
                        tops[j] = piece if tops[j] is None else jnp.maximum(tops[j], piece)
            top = jnp.max(jnp.concatenate(tops, axis=0), axis=-1, keepdims=True)
            top_v[b] = jnp.broadcast_to(top, (qrows, LANES))
            w = jnp.exp2(s_v[b] - jnp.maximum(top, floor_guard)).astype(jnp.bfloat16)
            wide_w = w.astype(jnp.float32)
            total = wide_w[:, :LANES]
            for c in range(1, span // LANES):
                total = total + wide_w[:, c * LANES:(c + 1) * LANES]
            acc = lax.dot_general(w, k_v[b, :latent, :], (((1,), (1,)), ((), ())),
                                  preferred_element_type=jnp.float32)
            tot_v[b] = jnp.broadcast_to(jnp.sum(total, axis=-1, keepdims=True), (qrows, LANES))
            acc_v[...] = acc
            for bit in range(2):
                @pl.when(core == bit)
                def _():
                    for j in range(draft):
                        for g in range(groups):
                            dst = keep_ref if g % 2 == bit else send_ref
                            at = j * heads + g * owned
                            for c in range(lat_tiles):
                                dst[g // 2, (b * draft + j) * lat_tiles + c] = acc_v[at:at + owned, c * LANES:(c + 1) * LANES]
        lane = lax.broadcasted_iota(jnp.int32, (owned, LANES), 1)
        for g in range(groups):
            stat = jnp.zeros((owned, LANES), jnp.float32)
            for r in range(count):
                b, j = r // draft, r % draft
                at = slice(j * heads + g * owned, j * heads + (g + 1) * owned)
                stat = jnp.where(lane == r, top_v[b, at, :], stat)
                stat = jnp.where(lane == count + r, tot_v[b, at, :], stat)
            stat_v[g] = stat
        for bit in range(2):
            @pl.when(core == bit)
            def _():
                for g in range(groups):
                    dst = keep_ref if g % 2 == bit else send_ref
                    dst[g // 2, tiles - 1] = stat_v[g]

    message = jax.ShapeDtypeStruct((pairs, tiles, owned, LANES), jnp.float32)
    any_space = pl.BlockSpec(memory_space=pl.ANY)
    return pl.pallas_call(
        kernel,
        out_shape=(message, message),
        in_specs=[any_space, any_space, pl.BlockSpec(memory_space=pltpu.SMEM)],
        out_specs=(pl.BlockSpec(memory_space=pltpu.VMEM),) * 2,
        scratch_shapes=[
            pltpu.VMEM((rows, draft, key_dim, heads), jnp.bfloat16),
            pltpu.VMEM((rows, key_dim, span), jnp.bfloat16),
            pltpu.VMEM((rows, qrows, span), jnp.float32),
            pltpu.VMEM((qrows, latent), jnp.float32),
            pltpu.VMEM((rows, qrows, LANES), jnp.float32),
            pltpu.VMEM((rows, qrows, LANES), jnp.float32),
            pltpu.VMEM((groups, owned, LANES), jnp.float32),
            pltpu.SemaphoreType.DMA((rows,)),
            pltpu.SemaphoreType.DMA((rows, FIRST_PARTS)),
        ],
        compiler_params=pltpu.CompilerParams(vmem_limit_bytes=51 << 20),
        name="attend",
    )(queries, cache, lengths)


def fold_stats(stats, count):
    peak = stats[0]
    for s in stats[1:]:
        peak = jnp.maximum(peak, s)
    scales = [jnp.exp2(s - peak) for s in stats]
    total = None
    for s, e in zip(stats, scales):
        part = pltpu.roll(s, LANES - count, 1) * e
        total = part if total is None else total + part
    lane = lax.broadcasted_iota(jnp.int32, peak.shape, 1)
    joint = jnp.where(lane < count, peak, pltpu.roll(total, count, 1))
    return scales, total, jnp.where(lane < 2 * count, joint, 0.0)


def add_cores(keep, other, count):
    pairs, tiles = keep.shape[:2]
    per = (tiles - 1) // count

    def kernel(a_ref, b_ref, o_ref):
        for a in range(a_ref.shape[0]):
            scales, _, joint = fold_stats([a_ref[a, tiles - 1], b_ref[a, tiles - 1]], count)
            o_ref[a, tiles - 1] = joint
            for r in range(count):
                ea = scales[0][:, r:r + 1]
                eb = scales[1][:, r:r + 1]
                for c in range(per):
                    t = r * per + c
                    o_ref[a, t] = a_ref[a, t] * ea + b_ref[a, t] * eb

    steps = 4
    spec = pl.BlockSpec((pairs // steps,) + keep.shape[1:], lambda i: (i, 0, 0, 0))
    return pl.pallas_call(
        kernel,
        grid=(steps,),
        out_shape=jax.ShapeDtypeStruct(keep.shape, jnp.float32),
        in_specs=[spec, spec],
        out_specs=spec,
        compiler_params=pltpu.CompilerParams(vmem_limit_bytes=32 << 20),
        name="add_cores",
    )(keep, other)


def up_project(parts, up_weight, count, copies):
    sources, tiles = parts.shape[:2]
    owned, latent, value_dim = up_weight.shape
    per = (tiles - 1) // count

    def kernel(p_ref, u_ref, o_ref, lat_v):
        scales, _, joint = fold_stats([p_ref[s, tiles - 1] for s in range(sources)], count)
        for r in range(count):
            es = [jnp.broadcast_to(e[:, r:r + 1], (SUB, LANES)) for e in scales]
            for c in range(per):
                t = r * per + c
                total = p_ref[0, t] * es[0]
                for s in range(1, sources):
                    total = total + p_ref[s, t] * es[s]
                lat_v[c, r * SUB:(r + 1) * SUB, :] = total
        row = lax.broadcasted_iota(jnp.int32, (count * SUB, value_dim), 0) % SUB
        lat = jnp.concatenate([lat_v[c] for c in range(per)], axis=1)
        values = jnp.zeros((count * SUB, value_dim), jnp.float32)
        for h in range(owned):
            values = jnp.where(row == h, split_dot(lat, u_ref[h]), values)
        for i in range(copies):
            for r in range(count):
                o_ref[i, r] = values[r * SUB:(r + 1) * SUB]
            o_ref[i, count] = joint

    return pl.pallas_call(
        kernel,
        out_shape=jax.ShapeDtypeStruct((copies, count + 1, SUB, LANES), jnp.float32),
        scratch_shapes=[pltpu.VMEM((per, count * SUB, LANES), jnp.float32)],
        compiler_params=pltpu.CompilerParams(vmem_limit_bytes=32 << 20),
        name="up_project",
    )(parts, up_weight)


def add_wide(parts, count, copies):
    sources = parts.shape[0]

    def kernel(p_ref, o_ref):
        scales, _, joint = fold_stats([p_ref[s, count] for s in range(sources)], count)
        for r in range(count):
            value = None
            for s in range(sources):
                part = p_ref[s, r] * scales[s][:, r:r + 1]
                value = part if value is None else value + part
            for i in range(copies):
                o_ref[i, r] = value
        for i in range(copies):
            o_ref[i, count] = joint

    return pl.pallas_call(
        kernel,
        out_shape=jax.ShapeDtypeStruct((copies,) + parts.shape[1:], jnp.float32),
        compiler_params=pltpu.CompilerParams(vmem_limit_bytes=32 << 20),
        name="add_wide",
    )(parts)


def out_project(parts, out_weight, count, copies):
    sources = parts.shape[0]
    features = out_weight.shape[0]

    def kernel(p_ref, w_ref, o_ref, val_v):
        scales, total, _ = fold_stats([p_ref[s, count] for s in range(sources)], count)
        inverse = 1.0 / total
        for r in range(count):
            value = None
            for s in range(sources):
                part = p_ref[s, r] * scales[s][:, r:r + 1]
                value = part if value is None else value + part
            val_v[r * SUB:(r + 1) * SUB, :] = value * inverse[:, r:r + 1]
        values = jnp.concatenate([val_v[pl.ds(h, count, stride=SUB), :] for h in range(SUB)], axis=1)
        mixed = split_dot(values, w_ref[...], 1)
        for i in range(copies):
            o_ref[i] = mixed

    return pl.pallas_call(
        kernel,
        out_shape=jax.ShapeDtypeStruct((copies, count, features), jnp.float32),
        scratch_shapes=[pltpu.VMEM((count * SUB, LANES), jnp.float32)],
        compiler_params=pltpu.CompilerParams(vmem_limit_bytes=32 << 20),
        name="out_project",
    )(parts, out_weight)


def body(queries, cache, lengths, up_weight, out_weight):
    rows, draft = queries.shape[:2]
    count = rows * draft
    groups = lax.axis_size("grp")
    wide = lax.axis_size("wide")
    near = 4
    same_core = [list(range(c, groups, 2)) for c in range(2)]
    along_y = [list(range(z, z + near)) for z in range(0, wide, near)]
    along_z = [list(range(y, wide, near)) for y in range(near)]
    keep, send = attend(jnp.swapaxes(queries, 2, 3), jnp.swapaxes(cache, 1, 2), lengths, groups, up_weight.shape[1])
    other = lax.ppermute(send, "grp", [(i, i ^ 1) for i in range(groups)])
    mine = add_cores(keep, other, count)
    parts = lax.all_to_all(mine, "grp", 0, 0, axis_index_groups=same_core, tiled=True)
    values = up_project(parts, up_weight, count, near)
    values = lax.all_to_all(values, "wide", 0, 0, axis_index_groups=along_y, tiled=True)
    values = add_wide(values, count, wide // near)
    values = lax.all_to_all(values, "wide", 0, 0, axis_index_groups=along_z, tiled=True)
    mixed = out_project(values, out_weight.T, count, groups)
    mixed = lax.all_to_all(mixed, "grp", 0, 0, tiled=True)
    return jnp.sum(mixed, axis=0).reshape(rows, draft, mixed.shape[2])


def solution(mesh):
    in_specs = (P(), P(None, ("grp", "wide"), None), P(), P("grp", None, None), P("grp", "wide"))
    out_specs = P(None, None, "wide")
    return jax.shard_map(body, mesh=mesh, in_specs=in_specs, out_specs=out_specs, check_vma=False)
```

```python
import math

import jax
import jax.numpy as jnp
from jax import lax
from jax.experimental import pallas as pl
from jax.experimental.pallas import tpu as pltpu
from jax.sharding import PartitionSpec as P

softmax_factor = 1.0 / math.sqrt(192.0) * (0.1 * math.log(40.0) + 1.0) ** 2
score_scale = softmax_factor * math.log2(math.e)
floor_value = -1e30
floor_guard = -5e29

LANES = 128
SUB = 8
FIRST_PART = 4


def split_dot(x, w, contract=0):
    rows = x.shape[0]
    high = x.astype(jnp.bfloat16)
    low = (x - high.astype(jnp.float32)).astype(jnp.bfloat16)
    both = lax.dot_general(jnp.concatenate([high, low], axis=0), w, (((1,), (contract,)), ((), ())),
                           preferred_element_type=jnp.float32)
    return both[:rows] + both[rows:]


def attend(queries, cache, lengths, groups, latent):
    rows, draft, key_dim, heads = queries.shape
    span = cache.shape[2]
    owned = heads // groups
    pairs = groups // 2
    lat_tiles = latent // LANES
    count = rows * draft
    tiles = count * lat_tiles + 1
    qrows = draft * heads

    def pieces(b):
        return [(0, span // FIRST_PART), (span // FIRST_PART, span)] if b == 0 else [(0, span)]

    def kernel(q_hbm, cache_hbm, len_ref, keep_ref, send_ref,
               q_v, k_v, s_v, acc_v, stat_v, q_sem, k_sem):
        grp = lax.axis_index("grp")
        core = lax.rem(grp, 2)
        start = (grp * lax.axis_size("wide") + lax.axis_index("wide")) * span
        q_copies = [pltpu.make_async_copy(q_hbm.at[b], q_v.at[b], q_sem.at[b]) for b in range(rows)]
        k_copies = [
            [pltpu.make_async_copy(cache_hbm.at[b, :, pl.ds(lo, hi - lo)], k_v.at[b, :, pl.ds(lo, hi - lo)], k_sem.at[b, p])
             for p, (lo, hi) in enumerate(pieces(b))] for b in range(rows)]
        for b in range(rows):
            q_copies[b].start()
            for copy in k_copies[b]:
                copy.start()
        lane = lax.broadcasted_iota(jnp.int32, (heads, LANES), 1)
        stat = jnp.zeros((heads, LANES), jnp.float32)
        for b in range(rows):
            q_copies[b].wait()
            tops = [None] * draft
            for copy, (lo, hi) in zip(k_copies[b], pieces(b)):
                copy.wait()
                pos = start + lo + lax.broadcasted_iota(jnp.int32, (1, hi - lo), 1)
                for j in range(draft):
                    s = lax.dot_general(q_v[b, j], k_v[b, :, lo:hi], (((0,), (0,)), ((), ())),
                                        preferred_element_type=jnp.float32) * score_scale
                    s = jnp.where(pos < len_ref[b] - draft + 1 + j, s, floor_value)
                    s_v[b, j * heads:(j + 1) * heads, lo:hi] = s
                    for c in range((hi - lo) // LANES):
                        piece = s[:, c * LANES:(c + 1) * LANES]
                        tops[j] = piece if tops[j] is None else jnp.maximum(tops[j], piece)
            top = jnp.max(jnp.concatenate(tops, axis=0), axis=-1, keepdims=True)
            w = jnp.exp2(s_v[b] - jnp.maximum(top, floor_guard)).astype(jnp.bfloat16)
            wide_w = w.astype(jnp.float32)
            total = wide_w[:, :LANES]
            for c in range(1, span // LANES):
                total = total + wide_w[:, c * LANES:(c + 1) * LANES]
            acc = lax.dot_general(w, k_v[b, :latent, :], (((1,), (1,)), ((), ())),
                                  preferred_element_type=jnp.float32)
            total = jnp.sum(total, axis=-1, keepdims=True)
            for j in range(draft):
                r = b * draft + j
                at = slice(j * heads, (j + 1) * heads)
                stat = jnp.where(lane == r, top[at], stat)
                stat = jnp.where(lane == count + r, total[at], stat)
            acc_v[...] = acc
            for bit in range(2):
                @pl.when(core == bit)
                def _():
                    for j in range(draft):
                        for g in range(groups):
                            dst = keep_ref if g % 2 == bit else send_ref
                            at = j * heads + g * owned
                            for c in range(lat_tiles):
                                dst[g // 2, (b * draft + j) * lat_tiles + c] = acc_v[at:at + owned, c * LANES:(c + 1) * LANES]
        stat_v[...] = stat
        for bit in range(2):
            @pl.when(core == bit)
            def _():
                for g in range(groups):
                    dst = keep_ref if g % 2 == bit else send_ref
                    dst[g // 2, tiles - 1] = stat_v[g * owned:(g + 1) * owned, :]

    message = jax.ShapeDtypeStruct((pairs, tiles, owned, LANES), jnp.float32)
    any_space = pl.BlockSpec(memory_space=pl.ANY)
    return pl.pallas_call(
        kernel,
        out_shape=(message, message),
        in_specs=[any_space, any_space, pl.BlockSpec(memory_space=pltpu.SMEM)],
        out_specs=(pl.BlockSpec(memory_space=pltpu.VMEM),) * 2,
        scratch_shapes=[
            pltpu.VMEM((rows, draft, key_dim, heads), jnp.bfloat16),
            pltpu.VMEM((rows, key_dim, span), jnp.bfloat16),
            pltpu.VMEM((rows, qrows, span), jnp.float32),
            pltpu.VMEM((qrows, latent), jnp.float32),
            pltpu.VMEM((heads, LANES), jnp.float32),
            pltpu.SemaphoreType.DMA((rows,)),
            pltpu.SemaphoreType.DMA((rows, 2)),
        ],
        compiler_params=pltpu.CompilerParams(vmem_limit_bytes=51 << 20),
        name="attend",
    )(queries, cache, lengths)


def fold_stats(stats, count):
    peak = stats[0]
    for s in stats[1:]:
        peak = jnp.maximum(peak, s)
    scales = [jnp.exp2(s - peak) for s in stats]
    total = None
    for s, e in zip(stats, scales):
        part = pltpu.roll(s, LANES - count, 1) * e
        total = part if total is None else total + part
    lane = lax.broadcasted_iota(jnp.int32, peak.shape, 1)
    joint = jnp.where(lane < count, peak, pltpu.roll(total, count, 1))
    return scales, total, jnp.where(lane < 2 * count, joint, 0.0)


def add_cores(keep, other, count):
    pairs, tiles = keep.shape[:2]
    per = (tiles - 1) // count

    def kernel(a_ref, b_ref, o_ref):
        for a in range(a_ref.shape[0]):
            scales, _, joint = fold_stats([a_ref[a, tiles - 1], b_ref[a, tiles - 1]], count)
            o_ref[a, tiles - 1] = joint
            for r in range(count):
                ea = scales[0][:, r:r + 1]
                eb = scales[1][:, r:r + 1]
                for c in range(per):
                    t = r * per + c
                    o_ref[a, t] = a_ref[a, t] * ea + b_ref[a, t] * eb

    return pl.pallas_call(
        kernel,
        out_shape=jax.ShapeDtypeStruct(keep.shape, jnp.float32),
        compiler_params=pltpu.CompilerParams(vmem_limit_bytes=32 << 20),
        name="add_cores",
    )(keep, other)


def up_project(parts, up_weight, count, copies):
    sources, tiles = parts.shape[:2]
    owned, latent, value_dim = up_weight.shape
    per = (tiles - 1) // count

    def kernel(p_ref, u_ref, o_ref, lat_v):
        scales, _, joint = fold_stats([p_ref[s, tiles - 1] for s in range(sources)], count)
        for r in range(count):
            es = [jnp.broadcast_to(e[:, r:r + 1], (SUB, LANES)) for e in scales]
            for c in range(per):
                t = r * per + c
                total = p_ref[0, t] * es[0]
                for s in range(1, sources):
                    total = total + p_ref[s, t] * es[s]
                lat_v[c, r * SUB:(r + 1) * SUB, :] = total
        row = lax.broadcasted_iota(jnp.int32, (count * SUB, value_dim), 0) % SUB
        lat = jnp.concatenate([lat_v[c] for c in range(per)], axis=1)
        values = jnp.zeros((count * SUB, value_dim), jnp.float32)
        for h in range(owned):
            values = jnp.where(row == h, split_dot(lat, u_ref[h]), values)
        for i in range(copies):
            for r in range(count):
                o_ref[i, r] = values[r * SUB:(r + 1) * SUB]
            o_ref[i, count] = joint

    return pl.pallas_call(
        kernel,
        out_shape=jax.ShapeDtypeStruct((copies, count + 1, SUB, LANES), jnp.float32),
        scratch_shapes=[pltpu.VMEM((per, count * SUB, LANES), jnp.float32)],
        compiler_params=pltpu.CompilerParams(vmem_limit_bytes=32 << 20),
        name="up_project",
    )(parts, up_weight)


def add_wide(parts, count, copies):
    sources = parts.shape[0]

    def kernel(p_ref, o_ref):
        scales, _, joint = fold_stats([p_ref[s, count] for s in range(sources)], count)
        for r in range(count):
            value = None
            for s in range(sources):
                part = p_ref[s, r] * scales[s][:, r:r + 1]
                value = part if value is None else value + part
            for i in range(copies):
                o_ref[i, r] = value
        for i in range(copies):
            o_ref[i, count] = joint

    return pl.pallas_call(
        kernel,
        out_shape=jax.ShapeDtypeStruct((copies,) + parts.shape[1:], jnp.float32),
        compiler_params=pltpu.CompilerParams(vmem_limit_bytes=32 << 20),
        name="add_wide",
    )(parts)


def out_project(parts, out_weight, count, copies):
    sources = parts.shape[0]
    features = out_weight.shape[0]

    def kernel(p_ref, w_ref, o_ref, val_v):
        scales, total, _ = fold_stats([p_ref[s, count] for s in range(sources)], count)
        inverse = 1.0 / total
        for r in range(count):
            value = None
            for s in range(sources):
                part = p_ref[s, r] * scales[s][:, r:r + 1]
                value = part if value is None else value + part
            val_v[r * SUB:(r + 1) * SUB, :] = value * inverse[:, r:r + 1]
        values = jnp.concatenate([val_v[pl.ds(h, count, stride=SUB), :] for h in range(SUB)], axis=1)
        mixed = split_dot(values, w_ref[...], 1)
        for i in range(copies):
            o_ref[i] = mixed

    return pl.pallas_call(
        kernel,
        out_shape=jax.ShapeDtypeStruct((copies, count, features), jnp.float32),
        scratch_shapes=[pltpu.VMEM((count * SUB, LANES), jnp.float32)],
        compiler_params=pltpu.CompilerParams(vmem_limit_bytes=32 << 20),
        name="out_project",
    )(parts, out_weight)


def body(queries, cache, lengths, up_weight, out_weight):
    rows, draft = queries.shape[:2]
    count = rows * draft
    groups = lax.axis_size("grp")
    wide = lax.axis_size("wide")
    near = 4
    same_core = [list(range(c, groups, 2)) for c in range(2)]
    along_y = [list(range(z, z + near)) for z in range(0, wide, near)]
    along_z = [list(range(y, wide, near)) for y in range(near)]
    keep, send = attend(jnp.swapaxes(queries, 2, 3), jnp.swapaxes(cache, 1, 2), lengths, groups, up_weight.shape[1])
    other = lax.ppermute(send, "grp", [(i, i ^ 1) for i in range(groups)])
    mine = add_cores(keep, other, count)
    parts = lax.all_to_all(mine, "grp", 0, 0, axis_index_groups=same_core, tiled=True)
    values = up_project(parts, up_weight, count, near)
    values = lax.all_to_all(values, "wide", 0, 0, axis_index_groups=along_y, tiled=True)
    values = add_wide(values, count, wide // near)
    values = lax.all_to_all(values, "wide", 0, 0, axis_index_groups=along_z, tiled=True)
    mixed = out_project(values, out_weight.T, count, groups)
    mixed = lax.all_to_all(mixed, "grp", 0, 0, tiled=True)
    return jnp.sum(mixed, axis=0).reshape(rows, draft, mixed.shape[2])


def solution(mesh):
    in_specs = (P(), P(None, ("grp", "wide"), None), P(), P("grp", None, None), P("grp", "wide"))
    out_specs = P(None, None, "wide")
    return jax.shard_map(body, mesh=mesh, in_specs=in_specs, out_specs=out_specs, check_vma=False)
```

```python
import math

import jax
import jax.numpy as jnp
from jax import lax
from jax.experimental import pallas as pl
from jax.experimental.pallas import tpu as pltpu
from jax.sharding import PartitionSpec as P

softmax_factor = 1.0 / math.sqrt(192.0) * (0.1 * math.log(40.0) + 1.0) ** 2
score_scale = softmax_factor * math.log2(math.e)
floor_value = -1e30
floor_guard = -5e29

LANES = 128
SUB = 8
FIRST_PART = 4


def split_dot(x, w, contract=0):
    rows = x.shape[0]
    high = x.astype(jnp.bfloat16)
    low = (x - high.astype(jnp.float32)).astype(jnp.bfloat16)
    both = lax.dot_general(jnp.concatenate([high, low], axis=0), w, (((1,), (contract,)), ((), ())),
                           preferred_element_type=jnp.float32)
    return both[:rows] + both[rows:]


def attend(queries, cache, lengths, groups, latent):
    rows, draft, key_dim, heads = queries.shape
    span = cache.shape[2]
    owned = heads // groups
    pairs = groups // 2
    lat_tiles = latent // LANES
    count = rows * draft
    tiles = count * lat_tiles + 1
    qrows = draft * heads

    def pieces(b):
        return [(0, span // FIRST_PART), (span // FIRST_PART, span)] if b == 0 else [(0, span)]

    def kernel(q_hbm, cache_hbm, len_ref, keep_ref, send_ref,
               q_v, k_v, s_v, acc_v, stat_v, q_sem, k_sem):
        grp = lax.axis_index("grp")
        core = lax.rem(grp, 2)
        start = (grp * lax.axis_size("wide") + lax.axis_index("wide")) * span
        q_copies = [pltpu.make_async_copy(q_hbm.at[b], q_v.at[b], q_sem.at[b]) for b in range(rows)]
        k_copies = [
            [pltpu.make_async_copy(cache_hbm.at[b, :, pl.ds(lo, hi - lo)], k_v.at[b, :, pl.ds(lo, hi - lo)], k_sem.at[b, p])
             for p, (lo, hi) in enumerate(pieces(b))] for b in range(rows)]
        for b in range(rows):
            q_copies[b].start()
            for copy in k_copies[b]:
                copy.start()
        lane = lax.broadcasted_iota(jnp.int32, (heads, LANES), 1)
        stat = jnp.zeros((heads, LANES), jnp.float32)
        for b in range(rows):
            if b == 0:
                q_copies[b].wait()
            tops = [None] * draft
            for copy, (lo, hi) in zip(k_copies[b], pieces(b)):
                if b == 0:
                    copy.wait()
                pos = start + lo + lax.broadcasted_iota(jnp.int32, (1, hi - lo), 1)
                for j in range(draft):
                    s = lax.dot_general(q_v[b, j], k_v[b, :, lo:hi], (((0,), (0,)), ((), ())),
                                        preferred_element_type=jnp.float32) * score_scale
                    s = jnp.where(pos < len_ref[b] - draft + 1 + j, s, floor_value)
                    s_v[b, j * heads:(j + 1) * heads, lo:hi] = s
                    for c in range((hi - lo) // LANES):
                        piece = s[:, c * LANES:(c + 1) * LANES]
                        tops[j] = piece if tops[j] is None else jnp.maximum(tops[j], piece)
            if b == 0:
                for later in range(1, rows):
                    for copy in [q_copies[later]] + k_copies[later]:
                        copy.wait()
            top = jnp.max(jnp.concatenate(tops, axis=0), axis=-1, keepdims=True)
            w = jnp.exp2(s_v[b] - jnp.maximum(top, floor_guard)).astype(jnp.bfloat16)
            wide_w = w.astype(jnp.float32)
            total = wide_w[:, :LANES]
            for c in range(1, span // LANES):
                total = total + wide_w[:, c * LANES:(c + 1) * LANES]
            acc = lax.dot_general(w, k_v[b, :latent, :], (((1,), (1,)), ((), ())),
                                  preferred_element_type=jnp.float32)
            total = jnp.sum(total, axis=-1, keepdims=True)
            for j in range(draft):
                r = b * draft + j
                at = slice(j * heads, (j + 1) * heads)
                stat = jnp.where(lane == r, top[at], stat)
                stat = jnp.where(lane == count + r, total[at], stat)
            acc_v[b] = acc
        stat_v[...] = stat
        for bit in range(2):
            @pl.when(core == bit)
            def _():
                for g in range(groups):
                    dst = keep_ref if g % 2 == bit else send_ref
                    dst[g // 2, tiles - 1] = stat_v[g * owned:(g + 1) * owned, :]
                    for r in range(count):
                        at = (r % draft) * heads + g * owned
                        for c in range(lat_tiles):
                            dst[g // 2, r * lat_tiles + c] = acc_v[r // draft, at:at + owned, c * LANES:(c + 1) * LANES]

    message = jax.ShapeDtypeStruct((pairs, tiles, owned, LANES), jnp.float32)
    any_space = pl.BlockSpec(memory_space=pl.ANY)
    return pl.pallas_call(
        kernel,
        out_shape=(message, message),
        in_specs=[any_space, any_space, pl.BlockSpec(memory_space=pltpu.SMEM)],
        out_specs=(pl.BlockSpec(memory_space=pltpu.VMEM),) * 2,
        scratch_shapes=[
            pltpu.VMEM((rows, draft, key_dim, heads), jnp.bfloat16),
            pltpu.VMEM((rows, key_dim, span), jnp.bfloat16),
            pltpu.VMEM((rows, qrows, span), jnp.float32),
            pltpu.VMEM((rows, qrows, latent), jnp.float32),
            pltpu.VMEM((heads, LANES), jnp.float32),
            pltpu.SemaphoreType.DMA((rows,)),
            pltpu.SemaphoreType.DMA((rows, 2)),
        ],
        compiler_params=pltpu.CompilerParams(vmem_limit_bytes=51 << 20),
        name="attend",
    )(queries, cache, lengths)


def fold_stats(stats, count):
    peak = stats[0]
    for s in stats[1:]:
        peak = jnp.maximum(peak, s)
    scales = [jnp.exp2(s - peak) for s in stats]
    total = None
    for s, e in zip(stats, scales):
        part = pltpu.roll(s, LANES - count, 1) * e
        total = part if total is None else total + part
    lane = lax.broadcasted_iota(jnp.int32, peak.shape, 1)
    joint = jnp.where(lane < count, peak, pltpu.roll(total, count, 1))
    return scales, total, jnp.where(lane < 2 * count, joint, 0.0)


def add_cores(keep, other, count):
    pairs, tiles = keep.shape[:2]
    per = (tiles - 1) // count

    def kernel(a_ref, b_ref, o_ref):
        for a in range(a_ref.shape[0]):
            scales, _, joint = fold_stats([a_ref[a, tiles - 1], b_ref[a, tiles - 1]], count)
            o_ref[a, tiles - 1] = joint
            for r in range(count):
                ea = scales[0][:, r:r + 1]
                eb = scales[1][:, r:r + 1]
                for c in range(per):
                    t = r * per + c
                    o_ref[a, t] = a_ref[a, t] * ea + b_ref[a, t] * eb

    return pl.pallas_call(
        kernel,
        out_shape=jax.ShapeDtypeStruct(keep.shape, jnp.float32),
        compiler_params=pltpu.CompilerParams(vmem_limit_bytes=32 << 20),
        name="add_cores",
    )(keep, other)


def up_project(parts, up_weight, count, copies):
    sources, tiles = parts.shape[:2]
    owned, latent, value_dim = up_weight.shape
    per = (tiles - 1) // count

    def kernel(p_ref, u_ref, o_ref, lat_v):
        scales, _, joint = fold_stats([p_ref[s, tiles - 1] for s in range(sources)], count)
        for r in range(count):
            es = [jnp.broadcast_to(e[:, r:r + 1], (SUB, LANES)) for e in scales]
            for c in range(per):
                t = r * per + c
                total = p_ref[0, t] * es[0]
                for s in range(1, sources):
                    total = total + p_ref[s, t] * es[s]
                lat_v[c, r * SUB:(r + 1) * SUB, :] = total
        row = lax.broadcasted_iota(jnp.int32, (count * SUB, value_dim), 0) % SUB
        lat = jnp.concatenate([lat_v[c] for c in range(per)], axis=1)
        values = jnp.zeros((count * SUB, value_dim), jnp.float32)
        for h in range(owned):
            values = jnp.where(row == h, split_dot(lat, u_ref[h]), values)
        for i in range(copies):
            for r in range(count):
                o_ref[i, r] = values[r * SUB:(r + 1) * SUB]
            o_ref[i, count] = joint

    return pl.pallas_call(
        kernel,
        out_shape=jax.ShapeDtypeStruct((copies, count + 1, SUB, LANES), jnp.float32),
        scratch_shapes=[pltpu.VMEM((per, count * SUB, LANES), jnp.float32)],
        compiler_params=pltpu.CompilerParams(vmem_limit_bytes=32 << 20),
        name="up_project",
    )(parts, up_weight)


def add_wide(parts, count, copies):
    sources = parts.shape[0]

    def kernel(p_ref, o_ref):
        scales, _, joint = fold_stats([p_ref[s, count] for s in range(sources)], count)
        for r in range(count):
            value = None
            for s in range(sources):
                part = p_ref[s, r] * scales[s][:, r:r + 1]
                value = part if value is None else value + part
            for i in range(copies):
                o_ref[i, r] = value
        for i in range(copies):
            o_ref[i, count] = joint

    return pl.pallas_call(
        kernel,
        out_shape=jax.ShapeDtypeStruct((copies,) + parts.shape[1:], jnp.float32),
        compiler_params=pltpu.CompilerParams(vmem_limit_bytes=32 << 20),
        name="add_wide",
    )(parts)


def out_project(parts, out_weight, count, copies):
    sources = parts.shape[0]
    features = out_weight.shape[0]

    def kernel(p_ref, w_ref, o_ref, val_v):
        scales, total, _ = fold_stats([p_ref[s, count] for s in range(sources)], count)
        inverse = 1.0 / total
        for r in range(count):
            value = None
            for s in range(sources):
                part = p_ref[s, r] * scales[s][:, r:r + 1]
                value = part if value is None else value + part
            val_v[r * SUB:(r + 1) * SUB, :] = value * inverse[:, r:r + 1]
        values = jnp.concatenate([val_v[pl.ds(h, count, stride=SUB), :] for h in range(SUB)], axis=1)
        mixed = split_dot(values, w_ref[...], 1)
        for i in range(copies):
            o_ref[i] = mixed

    return pl.pallas_call(
        kernel,
        out_shape=jax.ShapeDtypeStruct((copies, count, features), jnp.float32),
        scratch_shapes=[pltpu.VMEM((count * SUB, LANES), jnp.float32)],
        compiler_params=pltpu.CompilerParams(vmem_limit_bytes=32 << 20),
        name="out_project",
    )(parts, out_weight)


def body(queries, cache, lengths, up_weight, out_weight):
    rows, draft = queries.shape[:2]
    count = rows * draft
    groups = lax.axis_size("grp")
    wide = lax.axis_size("wide")
    near = 4
    same_core = [list(range(c, groups, 2)) for c in range(2)]
    along_y = [list(range(z, z + near)) for z in range(0, wide, near)]
    along_z = [list(range(y, wide, near)) for y in range(near)]
    keep, send = attend(jnp.swapaxes(queries, 2, 3), jnp.swapaxes(cache, 1, 2), lengths, groups, up_weight.shape[1])
    other = lax.ppermute(send, "grp", [(i, i ^ 1) for i in range(groups)])
    mine = add_cores(keep, other, count)
    parts = lax.all_to_all(mine, "grp", 0, 0, axis_index_groups=same_core, tiled=True)
    values = up_project(parts, up_weight, count, near)
    values = lax.all_to_all(values, "wide", 0, 0, axis_index_groups=along_y, tiled=True)
    values = add_wide(values, count, wide // near)
    values = lax.all_to_all(values, "wide", 0, 0, axis_index_groups=along_z, tiled=True)
    mixed = out_project(values, out_weight.T, count, groups)
    mixed = lax.all_to_all(mixed, "grp", 0, 0, tiled=True)
    return jnp.sum(mixed, axis=0).reshape(rows, draft, mixed.shape[2])


def solution(mesh):
    in_specs = (P(), P(None, ("grp", "wide"), None), P(), P("grp", None, None), P("grp", "wide"))
    out_specs = P(None, None, "wide")
    return jax.shard_map(body, mesh=mesh, in_specs=in_specs, out_specs=out_specs, check_vma=False)
```
